128 devices in a mesh: row: 8 (over x_hi, y), col: 8 (over z, x_lo), layer: 2 (over core).
Axes of the slice: x: 4 (x_hi: 2, x_lo: 2; x = x_hi * 2 + x_lo), y: 4, z: 4, core: 2. Of those that a mesh axis runs over, the one named last changes fastest.
Arguments:
- points: float32 [3, 131072], P(None, ('row', 'col', 'layer')), may hold values from 0 to 1
- counts: int32 [131072], P(('row', 'col', 'layer')), may hold values from 0 to 29
- latent: float32 [131072], P(('row', 'col', 'layer')), may hold values from -4 to 4
- probes: float32 [16, 131072], P(None, ('row', 'col', 'layer')), may hold values from -6 to 6
Outputs:
- applied: float32 [16, 131072], P(None, ('row', 'col', 'layer'))
The draws below stay inside these ranges and needn't reach their ends.
All inputs are finite; a program needn't handle non-finite values.
Results may differ from the reference program's by a relative error of at most 0.0011.
Values may be sent and summed in bfloat16 or wider, within the bound.
A program may use at most 64 MiB of HBM per device.

```python
import jax
import jax.numpy as jnp
from jax import lax

PROBES = 16
DIMS = 3
NPTS = 131072


def set_ends(entries, stream_key, least, largest):
    dims = entries.shape
    spot = [jax.random.randint(jax.random.fold_in(stream_key, axis), (), 0, dims[axis]) for axis in range(len(dims))]
    entries = entries.at[tuple(spot)].set(least)
    longest = dims.index(max(dims))
    spot[longest] = (spot[longest] + 1) % dims[longest]
    return entries.at[tuple(spot)].set(largest)


def shard_levels(key, shape, cuts, low, high):
    factor_of = 1.0
    for axis_at, blocks in cuts:
        steps = jax.random.uniform(jax.random.fold_in(jax.random.fold_in(key, 6), axis_at), (blocks,), jnp.float32, low / len(cuts), high / len(cuts))
        factor_of = factor_of * jnp.repeat(jnp.exp(steps), shape[axis_at] // blocks).reshape((-1,) + (1,) * (len(shape) - 1 - axis_at))
    return factor_of


def bell_draw(key, dims, spread, most, cuts=(), held_as=jnp.bfloat16):
    factor_of = shard_levels(key, dims, cuts, -0.22, 0.18) if cuts else 1.0
    result = jax.random.normal(key, dims, jnp.float32) * spread * factor_of
    return jnp.minimum(jnp.maximum(result, -most), most).astype(held_as)


def setup_inputs(seed: int = 0) -> dict:
    seeds = jax.random.split(jax.random.key(seed), 5)
    points = jnp.clip(1.0 * jax.random.uniform(seeds[0], (DIMS, NPTS), jnp.float32) ** shard_levels(seeds[0], (DIMS, NPTS), ((1, 128),), -0.2, 0.2), 0.0, 1.0)
    counts = set_ends(jax.random.randint(seeds[1], (NPTS,), 0, 30), jax.random.fold_in(seeds[1], 1), 0, 29).astype(jnp.int32)
    latent = bell_draw(seeds[2], (NPTS,), 1.0, 4.0, ((0, 128),), jnp.float32)
    probes = bell_draw(seeds[3], (PROBES, NPTS), 1.0, 6.0, ((1, 128),), jnp.float32)
    return dict(points=points, counts=counts, latent=latent, probes=probes)


LENGTH = 0.25
AMP = 0.02
DISP = 4.0

def kernel_block(row_pts, col_pts):
    d2 = (row_pts[0][:, None] - col_pts[0][None, :]) ** 2
    d2 = d2 + (row_pts[1][:, None] - col_pts[1][None, :]) ** 2
    d2 = d2 + (row_pts[2][:, None] - col_pts[2][None, :]) ** 2
    scaled = jnp.sqrt(d2) * (jnp.sqrt(5.0) / LENGTH)
    return (AMP * (1.0 + scaled + scaled * scaled / 3.0) * jnp.exp(-scaled)).astype(jnp.bfloat16)

def reference(points, counts, latent, probes):
    mean_val = jnp.exp(latent)
    weight = DISP * mean_val * (DISP + counts.astype(jnp.float32)) / (DISP + mean_val) ** 2
    root = jnp.sqrt(weight)
    carried = (root[None, :] * probes).astype(jnp.bfloat16)
    total = points.shape[1]
    block = 256
    blocks = points.reshape(3, total // block, block).transpose(1, 0, 2)

    def one_block(row_pts):
        kernel = kernel_block(row_pts, points)
        return jnp.dot(kernel, carried.T, preferred_element_type=jnp.float32)
    parts = lax.map(one_block, blocks)
    summed = parts.reshape(total, PROBES).T
    return probes + root[None, :] * summed
```

```python
import functools
import math

import jax
import jax.numpy as jnp
from jax import lax
from jax.experimental import pallas as pl
from jax.experimental.pallas import tpu as pltpu
from jax.sharding import PartitionSpec as P

LENGTH = 0.25
AMP = 0.02
DISP = 4.0

MESH = pl.DeviceIdType.MESH
SH = 1024
BI, BJ = 512, 256
DEPTH = 8
FEAT = 64

L2E = math.log2(math.e)
COORD = math.sqrt(5.0) / LENGTH * L2E
H = 1.5 * L2E
D = 0.75 * L2E * L2E
B0 = math.log2(AMP / (3.0 * L2E * L2E))
FLOOR = 3e-5


def entries(u):
    s = u * lax.rsqrt(jnp.maximum(u, FLOOR))
    t = s + H
    return ((t * t + D) * jnp.exp2(B0 - s)).astype(jnp.bfloat16)


def pieces(v):
    high = v.astype(jnp.bfloat16).astype(jnp.float32)
    rest = v - high
    mid = rest.astype(jnp.bfloat16).astype(jnp.float32)
    return high, mid, rest - mid


def features(pts):
    a = (pts - 0.5) * COORD
    norm = jnp.sum(a * a, axis=0, keepdims=True)
    h, m, l = pieces(a)
    nh, nm, nl = pieces(norm)
    at = lax.broadcasted_iota(jnp.int32, a.shape, 0)
    ones = jnp.where(at < 3, 1.0, 0.0)
    sq = jnp.where(at == 0, nh, jnp.where(at == 1, nm, jnp.where(at == 2, nl, 0.0)))
    left = jnp.concatenate([h, h, m, m, h, l, sq, ones], axis=0)
    right = jnp.concatenate([-2.0 * h, -2.0 * m, -2.0 * h, -2.0 * m, -2.0 * l, -2.0 * h, ones, sq], axis=0)
    return left, right


def kernel(groups, members, pts, cnt, lat, prb, out, xs, cs, fi, fj, sums, parts, own, *rest):
    us, ks = rest[:DEPTH], rest[DEPTH : 2 * DEPTH]
    xsend, csend, xrecv, crecv, psend, precv = rest[2 * DEPTH :]
    row, col, layer = lax.axis_index("row"), lax.axis_index("col"), lax.axis_index("layer")
    a = row * 2 + lax.rem(col, 2)
    m = lax.div(col, 2) * 2 + layer
    b = lax.rem(a + m + 1, groups)

    def dev(group, member):
        return (lax.div(group, 2), lax.div(member, 2) * 2 + lax.rem(group, 2), lax.rem(member, 2))

    def mate(k):
        return lax.rem(m + k, members)

    def asker(k):
        return dev(lax.rem(a + groups - k - 1, groups), jnp.int32(k))

    def cols(j):
        return pl.ds(pl.multiple_of(j * SH, SH), SH)

    barrier = pltpu.get_barrier_semaphore()
    for k in range(1, members):
        pl.semaphore_signal(barrier, inc=1, device_id=dev(a, mate(k)), device_id_type=MESH)
    for k in range(members):
        pl.semaphore_signal(barrier, inc=1, device_id=asker(k), device_id_type=MESH)
    for k in range(members):
        pl.semaphore_signal(barrier, inc=1, device_id=dev(b, jnp.int32(k)), device_id_type=MESH)

    mean_val = jnp.exp(lat[...])
    weight = DISP * mean_val * (DISP + cnt[...].astype(jnp.float32)) / (DISP + mean_val) ** 2
    root = jnp.sqrt(weight)
    cs[0, :, cols(m)] = (root * prb[...]).astype(jnp.bfloat16)
    xs[0, m] = jnp.full((8, SH), 0.5, jnp.float32)
    xs[0, m, 0:3, :] = pts[...]
    sums[...] = jnp.zeros_like(sums)
    for k in ks:
        k[...] = jnp.zeros_like(k)

    pl.semaphore_wait(barrier, 3 * members - 1)

    sends = []

    def send(src, dst, ssem, rsem, to):
        copy = pltpu.make_async_remote_copy(
            src_ref=src, dst_ref=dst, send_sem=ssem, recv_sem=rsem, device_id=to, device_id_type=MESH
        )
        copy.start()
        sends.append(copy)

    def shard(which, to, n):
        send(xs.at[0, m], xs.at[which, m], xsend.at[n], xrecv.at[which, m], to)
        send(cs.at[0, :, cols(m)], cs.at[which, :, cols(m)], csend.at[n], crecv.at[which, m], to)

    for k in range(members):
        shard(1, asker(k), k)
        if k:
            shard(0, dev(a, mate(k)), members + k - 1)

    def arrived(ref, sem):
        pltpu.make_async_remote_copy(
            src_ref=ref, dst_ref=ref, send_sem=psend.at[0], recv_sem=sem, device_id=dev(a, mate(1)), device_id_type=MESH
        ).wait_recv()

    def build(which, j):
        left, right = features(xs[which, j])
        fi[which, cols(j), :] = left.T.astype(jnp.bfloat16)
        fj[which, :, cols(j)] = right.astype(jnp.bfloat16)

    build(0, m)
    for blk in range(SH // BI):
        for half in range(BI // BJ):
            at = blk * BI + half * BJ
            rows = pl.ds(pl.multiple_of(m * SH + blk * BI, BI), BI)
            at_cols = pl.ds(pl.multiple_of(m * SH + at, BJ), BJ)
            k = entries(jnp.dot(fi[0, rows, :], fj[0, :, at_cols], preferred_element_type=jnp.float32))
            own[:, at : at + BJ] = jnp.dot(cs[0, :, rows], k, preferred_element_type=jnp.float32)

    for k in range(members):
        if k:
            arrived(xs.at[0, mate(k)], xrecv.at[0, mate(k)])
            arrived(cs.at[0, :, cols(mate(k))], crecv.at[0, mate(k)])
            build(0, mate(k))
        arrived(xs.at[1, k], xrecv.at[1, k])
        arrived(cs.at[1, :, cols(k)], crecv.at[1, k])
        build(1, k)

    ni, nj = members * SH // BI, members * SH // BJ
    inside = jnp.logical_and(m == members - 1, a >= members)
    per = 2 * (ni - 1)
    half_count = (ni // 2) * per
    count = jnp.where(inside, 2 * half_count, ni * nj)

    def place(t):
        t = jnp.minimum(jnp.maximum(t, 0), count - 1)
        j0, i0 = lax.div(t, ni), lax.rem(t, ni)
        side = lax.div(t, half_count)
        r = t - side * half_count
        g = lax.div(r, per)
        r = r - g * per
        n1 = 2 * (ni - 1 - g)
        i1 = jnp.where(r < n1, g, ni - 1 - g)
        j1 = 2 * i1 + 2 + jnp.where(r < n1, r, r - n1)
        i, j = jnp.where(inside, i1, i0), jnp.where(inside, j1, j0)
        si, sj = jnp.where(inside, side, 0), jnp.where(inside, side, 1)
        return si, pl.ds(pl.multiple_of(i * BI, BI), BI), sj, pl.ds(pl.multiple_of(j * BJ, BJ), BJ)

    def distance(t, u):
        si, rows, sj, at_cols = place(t)
        u[...] = jnp.dot(fi[si, rows, :], fj[sj, :, at_cols], preferred_element_type=jnp.float32)

    def products(t, k):
        si, rows, sj, at_cols = place(t)
        kv = k[...]
        sums[sj, :, at_cols] += jnp.dot(cs[si, :, rows], kv, preferred_element_type=jnp.float32)
        sums[si, :, rows] += lax.dot_general(
            cs[sj, :, at_cols], kv, (((1,), (1,)), ((), ())), preferred_element_type=jnp.float32
        )

    distance(jnp.int32(0), us[0])

    def step(p, carry):
        t = p * DEPTH
        for n in range(DEPTH):
            distance(t + n + 1, us[(n + 1) % DEPTH])
            products(t + n - 1, ks[(n - 1) % DEPTH])
            ks[n][...] = entries(us[n][...])
        return carry

    lax.fori_loop(0, lax.div(count, DEPTH), step, 0)
    products(count - 1, ks[DEPTH - 1])

    for k in range(members):
        send(sums.at[1, :, cols(k)], parts.at[members + m], psend.at[k], precv.at[members + m], dev(b, jnp.int32(k)))
        if k:
            send(sums.at[0, :, cols(mate(k))], parts.at[m], psend.at[members + k - 1], precv.at[m], dev(a, mate(k)))
    total = own[...] + sums[0, :, cols(m)]
    for k in range(members):
        arrived(parts.at[members + k], precv.at[members + k])
        total = total + parts[members + k]
        if k:
            arrived(parts.at[mate(k)], precv.at[mate(k)])
            total = total + parts[mate(k)]
    out[...] = prb[...] + root * total
    for copy in sends:
        copy.wait_send()


def local(groups, members, points, counts, latent, probes):
    size = members * SH
    vmem = pl.BlockSpec(memory_space=pltpu.VMEM)
    copies = 2 * members - 1
    return pl.pallas_call(
        functools.partial(kernel, groups, members),
        out_shape=jax.ShapeDtypeStruct(probes.shape, jnp.float32),
        in_specs=[vmem] * 4,
        out_specs=vmem,
        scratch_shapes=[
            pltpu.VMEM((2, members, 8, SH), jnp.float32),
            pltpu.VMEM((2, 16, size), jnp.bfloat16),
            pltpu.VMEM((2, size, FEAT), jnp.bfloat16),
            pltpu.VMEM((2, FEAT, size), jnp.bfloat16),
            pltpu.VMEM((2, 16, size), jnp.float32),
            pltpu.VMEM((2 * members, 16, SH), jnp.float32),
            pltpu.VMEM((16, SH), jnp.float32),
            *[pltpu.VMEM((BI, BJ), jnp.float32)] * DEPTH,
            *[pltpu.VMEM((BI, BJ), jnp.bfloat16)] * DEPTH,
            pltpu.SemaphoreType.DMA((copies,)),
            pltpu.SemaphoreType.DMA((copies,)),
            pltpu.SemaphoreType.DMA((2, members)),
            pltpu.SemaphoreType.DMA((2, members)),
            pltpu.SemaphoreType.DMA((copies,)),
            pltpu.SemaphoreType.DMA((2 * members,)),
        ],
        compiler_params=pltpu.CompilerParams(
            collective_id=0, has_side_effects=True, vmem_limit_bytes=48 * 2**20
        ),
        cost_estimate=pl.CostEstimate(flops=10**10, bytes_accessed=10**7, transcendentals=10**8),
    )(points, counts.reshape(1, SH), latent.reshape(1, SH), probes)


def solution(mesh):
    spec = ("row", "col", "layer")
    groups = mesh.shape["row"] * 2
    members = mesh.shape["col"] // 2 * mesh.shape["layer"]
    return jax.shard_map(
        functools.partial(local, groups, members),
        mesh=mesh,
        in_specs=(P(None, spec), P(spec), P(spec), P(None, spec)),
        out_specs=P(None, spec),
        check_vma=False,
    )
```

```python
import functools
import math

import jax
import jax.numpy as jnp
from jax import lax
from jax.experimental import pallas as pl
from jax.experimental.pallas import tpu as pltpu
from jax.sharding import PartitionSpec as P

LENGTH = 0.25
AMP = 0.02
DISP = 4.0

MESH = pl.DeviceIdType.MESH
SH = 1024
BI, BJ = 512, 256
DEPTH = 8
AHEAD = 5
FEAT = 48

L2E = math.log2(math.e)
COORD = math.sqrt(5.0) / LENGTH * L2E
H = 1.5 * L2E
D = 0.75 * L2E * L2E
B0 = math.log2(AMP / (3.0 * L2E * L2E))
FLOOR = 3e-5


def entries(u):
    s = u * lax.rsqrt(jnp.maximum(u, FLOOR))
    t = s + H
    return ((t * t + D) * jnp.exp2(B0 - s)).astype(jnp.bfloat16)


def pieces(v):
    high = v.astype(jnp.bfloat16).astype(jnp.float32)
    rest = v - high
    mid = rest.astype(jnp.bfloat16).astype(jnp.float32)
    return high, mid, rest - mid


def packed(pts):
    a = (pts - 0.5) * COORD
    at = lax.broadcasted_iota(jnp.int32, a.shape, 0)
    h, m, l = (jnp.where(at < 3, v, 0.0) for v in pieces(a))
    return jnp.concatenate([h + jnp.roll(m, 4, axis=0), l], axis=0).astype(jnp.bfloat16)


def features(packs):
    both = packs.astype(jnp.float32)
    hm, low = both[:8], both[8:]
    mh = jnp.roll(hm, 4, axis=0)
    at = lax.broadcasted_iota(jnp.int32, hm.shape, 0)
    a = jnp.where(at < 3, hm + mh + low, 0.0)
    nh, nm, nl = pieces(jnp.sum(a * a, axis=0, keepdims=True))
    ones = jnp.where(at < 3, 1.0, 0.0)
    sq = jnp.where(at == 0, nh, jnp.where(at == 1, nm, jnp.where(at == 2, nl, 0.0)))
    left = jnp.concatenate([hm, hm, hm, low, sq, ones], axis=0)
    right = jnp.concatenate([-2.0 * hm, -2.0 * mh, -2.0 * low, -2.0 * hm, ones, sq], axis=0)
    return left, right


def plan(members):
    half = members // 2
    shells = []
    for k in range(half):
        shells += [(i, k) for i in range(k)] + [(k, j) for j in range(k + 1)]
    top = members - 1
    pairs = shells + [(i, j) for i in range(half) for j in range(half, members)]
    pairs += [(i, j) for j in range(half) for i in range(half, members)]
    pairs += [(top - i, top - j) for i, j in reversed(shells)]
    outside = [(0, i, 1, j) for i, j in pairs]
    inside = []
    for k in range(1, half):
        for side in (1, 0):
            inside += [(side, i, side, k) for i in range(k)]
    for side in (1, 0):
        inside += [(side, i, side, j) for i in range(members) for j in range(max(half, i + 1), members)]
    first = len(outside) - len(inside)
    inside = [None] * first + inside

    def uses(cells, shard):
        return [n for n, cell in enumerate(cells) if cell and shard in (cell[:2], cell[2:])]

    shards = [(1, k) for k in range(members)] + [(0, k) for k in range(1, members)]
    take = {shard: uses(outside, shard)[0] - 1 for shard in shards}
    order = sorted(shards, key=lambda shard: (take[shard], shard))
    for shard in order[1:]:
        assert first == 0 or take[shard] < first or take[shard] < uses(inside, shard)[0]
    send = {shard: 2 * (n - AHEAD) if n >= AHEAD else -1 for n, shard in enumerate(order)}
    give = []
    for cells in (outside, inside):
        steps, at = {}, 0
        for last, shard in sorted((uses(cells, shard)[-1], shard) for shard in shards):
            at = max(last + 1, at + 1)
            steps[shard] = at
        give.append(steps)
    return outside, inside, first, order, take, send, give


def kernel(groups, members, pts_hbm, cnt_hbm, lat_hbm, prb_hbm, out, pts, cnt, lat, prb, xs, fi, fj, sums, parts, own, *rest):
    us, ks = rest[:DEPTH], rest[DEPTH : 2 * DEPTH]
    load, xsend, xrecv, psend, precv = rest[2 * DEPTH :]
    row, col, layer = lax.axis_index("row"), lax.axis_index("col"), lax.axis_index("layer")
    a = row * 2 + lax.rem(col, 2)
    m = lax.div(col, 2) * 2 + layer
    b = lax.rem(a + m + 1, groups)

    def dev(group, member):
        return (lax.div(group, 2), lax.div(member, 2) * 2 + lax.rem(group, 2), lax.rem(member, 2))

    def mate(k):
        return lax.rem(m + k, members)

    def back(k):
        return lax.rem(m + members - k, members)

    def asker(k):
        return dev(lax.rem(a + groups - k - 1, groups), k)

    def cols(j):
        return pl.ds(pl.multiple_of(j * SH, SH), SH)

    pts[...] = jnp.zeros_like(pts)
    loads = [
        pltpu.make_async_copy(src, dst, load.at[n])
        for n, (src, dst) in enumerate([(pts_hbm, pts.at[0:3]), (cnt_hbm, cnt), (lat_hbm, lat), (prb_hbm, prb)])
    ]
    for copy in loads:
        copy.start()
    barrier = pltpu.get_barrier_semaphore()
    for k in range(members):
        pl.semaphore_signal(barrier, inc=1, device_id=dev(b, back(k)), device_id_type=MESH)
    for k in range(1, members):
        pl.semaphore_signal(barrier, inc=1, device_id=dev(a, mate(k)), device_id_type=MESH)

    sums[...] = jnp.zeros_like(sums)
    for k in ks:
        k[...] = jnp.zeros_like(k)
    for copy in loads:
        copy.wait()

    mean_val = jnp.exp(lat[...])
    weight = DISP * mean_val * (DISP + cnt[...].astype(jnp.float32)) / (DISP + mean_val) ** 2
    root = jnp.sqrt(weight)
    xs[0, m, 0:16, :] = (root * prb[...]).astype(jnp.bfloat16)
    xs[0, m, 16:32, :] = packed(pts[...])

    def build(which, j):
        left, right = features(xs[which, j, 16:32, :])
        fi[which, cols(j), :] = left.T.astype(jnp.bfloat16)
        fj[which, :, cols(j)] = right.astype(jnp.bfloat16)

    build(0, m)
    for first in range(0, SH, BI):
        rows = pl.ds(pl.multiple_of(m * SH + first, BI), BI)
        for at in range(first, SH, BJ):
            at_cols = pl.ds(pl.multiple_of(m * SH + at, BJ), BJ)
            k = entries(jnp.dot(fi[0, rows, :], fj[0, :, at_cols], preferred_element_type=jnp.float32))
            term = jnp.dot(xs[0, m, 0:16, first : first + BI], k, preferred_element_type=jnp.float32)
            if first == 0:
                own[:, at : at + BJ] = term
            else:
                own[:, at : at + BJ] += term
            if at >= first + BI:
                own[:, first : first + BI] += lax.dot_general(
                    xs[0, m, 0:16, at : at + BJ], k, (((1,), (1,)), ((), ())), preferred_element_type=jnp.float32
                )

    pl.semaphore_wait(barrier, 2 * members - 1)

    def remote(src, dst, ssem, rsem, to):
        return pltpu.make_async_remote_copy(
            src_ref=src, dst_ref=dst, send_sem=ssem, recv_sem=rsem, device_id=to, device_id_type=MESH
        )

    def ask(k):
        return remote(xs.at[0, m], xs.at[1, m], xsend.at[k], xrecv.at[1, m], asker(mate(k)))

    def share(k):
        return remote(xs.at[0, m], xs.at[0, m], xsend.at[members - 1 + k], xrecv.at[0, m], dev(a, back(k)))

    outside_cells, inside_cells, first_inside, order, take_at, send_at, give_at = plan(members)
    steps = len(outside_cells)

    for which, k in order[:AHEAD]:
        (ask if which else share)(k).start()

    def arrived(ref, sem):
        remote(ref, ref, psend.at[0], sem, dev(a, mate(1))).wait_recv()

    def take(which, j):
        arrived(xs.at[which, j], xrecv.at[which, j])
        build(which, j)

    inside = jnp.logical_and(m == members - 1, a >= members)
    start = jnp.where(inside, first_inside, 0)

    def look(at, table):
        found = jnp.int32(0)
        for n, value in table.items():
            found = jnp.where(at == n, value, found)
        return found

    def code(which, k):
        return which * members + k

    cells = {}
    for kind, listed in enumerate((outside_cells, inside_cells)):
        for n, at in enumerate(listed):
            if at is not None:
                cells[n + kind * steps] = code(*at[:2]) * 2 * members + code(*at[2:])

    def shard_of(value):
        which = lax.div(value, members)
        k = lax.rem(value, members)
        return which, jnp.where(which == 0, mate(k), back(k))

    kind_at = jnp.where(inside, steps, 0)

    def cell(c):
        return look(jnp.minimum(c, steps - 1) + kind_at, cells)

    def place(at, n):
        si, i = shard_of(lax.div(at, 2 * members))
        sj, j = shard_of(lax.rem(at, 2 * members))
        first, second = (n % (SH // BI)) * BI, (n // (SH // BI)) * BJ
        rows = pl.ds(pl.multiple_of(i * SH + first, BI), BI)
        at_cols = pl.ds(pl.multiple_of(j * SH + second, BJ), BJ)
        return si, rows, sj, at_cols, xs.at[si, i, 0:16, first : first + BI], xs.at[sj, j, 0:16, second : second + BJ]

    def distance(at, n, u):
        si, rows, sj, at_cols, _, _ = place(at, n)
        u[...] = jnp.dot(fi[si, rows, :], fj[sj, :, at_cols], preferred_element_type=jnp.float32)

    def products(at, n, k):
        si, rows, sj, at_cols, ci, cj = place(at, n)
        kv = k[...]
        sums[sj, :, at_cols] += jnp.dot(ci[...], kv, preferred_element_type=jnp.float32)
        sums[si, :, rows] += lax.dot_general(
            cj[...], kv, (((1,), (1,)), ((), ())), preferred_element_type=jnp.float32
        )

    def give_row(k):
        j = mate(k)
        return remote(sums.at[0, :, cols(j)], parts.at[m], psend.at[k - 1], precv.at[m], dev(a, j))

    def give_col(k):
        j = back(k)
        return remote(sums.at[1, :, cols(j)], parts.at[members + m], psend.at[members - 1 + k], precv.at[members + m], dev(b, j))

    sending = {send_at[shard]: code(*shard) + 1 for shard in order[AHEAD:]}
    taking = {take_at[shard]: code(*shard) + 1 for shard in order[1:]}
    giving = {}
    for kind, table in enumerate(give_at):
        for shard, n in table.items():
            if n < steps - 1:
                giving[n + 1 + kind * steps] = code(*shard) + 1

    def due(c):
        return look(c, sending), look(c, taking), look(c + kind_at, giving)

    def transfers(send, arrival, give):
        @pl.when(send + arrival + give > 0)
        def _():
            @pl.when(give > members)
            def _():
                give_col(give - 1 - members).start()

            @pl.when(jnp.logical_and(give > 0, give <= members))
            def _():
                give_row(give - 1).start()

            @pl.when(send > members)
            def _():
                ask(send - 1 - members).start()

            @pl.when(jnp.logical_and(send > 0, send <= members))
            def _():
                share(send - 1).start()

            @pl.when(arrival > 0)
            def _():
                take(*shard_of(arrival - 1))

    def early(c, carry):
        transfers(look(c, sending), look(c, taking), jnp.int32(0))
        return carry

    take(1, back(0))
    lax.fori_loop(0, start, early, 0)
    begin = cell(start)
    distance(begin, 0, us[0])

    def step(c, carry):
        last, this, *events = carry
        transfers(*events)
        after = cell(c + 1)
        for n in range(DEPTH):
            if n == DEPTH - 1:
                distance(after, 0, us[0])
            else:
                distance(this, n + 1, us[n + 1])
            if n == 0:
                products(last, DEPTH - 1, ks[DEPTH - 1])
            else:
                products(this, n - 1, ks[n - 1])
            ks[n][...] = entries(us[n][...])

        return (this, after, *due(c + 1))

    last, *_ = lax.fori_loop(start, steps, step, (begin, begin, *due(start)))
    products(last, DEPTH - 1, ks[DEPTH - 1])
    for kind, table in enumerate(give_at):
        for (which, k), n in table.items():
            if n >= steps - 1:

                @pl.when(inside if kind else jnp.logical_not(inside))
                def _(which=which, k=k):
                    (give_col if which else give_row)(k).start()

    total = own[...] + sums[0, :, cols(m)]
    for k in range(members):
        arrived(parts.at[members + k], precv.at[members + k])
        total = total + parts[members + k]
        if k:
            arrived(parts.at[back(k)], precv.at[back(k)])
            total = total + parts[back(k)]
    out[...] = prb[...] + root * total
    for k in range(members):
        ask(k).wait_send()
        give_col(k).wait_send()
        if k:
            share(k).wait_send()
            give_row(k).wait_send()


def local(groups, members, points, counts, latent, probes):
    assert DEPTH == (SH // BI) * (SH // BJ)
    size = members * SH
    copies = 2 * members - 1
    return pl.pallas_call(
        functools.partial(kernel, groups, members),
        out_shape=jax.ShapeDtypeStruct(probes.shape, jnp.float32),
        in_specs=[pl.BlockSpec(memory_space=pl.ANY)] * 4,
        out_specs=pl.BlockSpec(memory_space=pltpu.VMEM),
        scratch_shapes=[
            pltpu.VMEM((8, SH), jnp.float32),
            pltpu.VMEM((1, SH), jnp.int32),
            pltpu.VMEM((1, SH), jnp.float32),
            pltpu.VMEM((16, SH), jnp.float32),
            pltpu.VMEM((2, members, 32, SH), jnp.bfloat16),
            pltpu.VMEM((2, size, FEAT), jnp.bfloat16),
            pltpu.VMEM((2, FEAT, size), jnp.bfloat16),
            pltpu.VMEM((2, 16, size), jnp.float32),
            pltpu.VMEM((2 * members, 16, SH), jnp.float32),
            pltpu.VMEM((16, SH), jnp.float32),
            *[pltpu.VMEM((BI, BJ), jnp.float32)] * DEPTH,
            *[pltpu.VMEM((BI, BJ), jnp.bfloat16)] * DEPTH,
            pltpu.SemaphoreType.DMA((4,)),
            pltpu.SemaphoreType.DMA((copies,)),
            pltpu.SemaphoreType.DMA((2, members)),
            pltpu.SemaphoreType.DMA((copies,)),
            pltpu.SemaphoreType.DMA((2 * members,)),
        ],
        compiler_params=pltpu.CompilerParams(
            collective_id=0, has_side_effects=True, vmem_limit_bytes=48 * 2**20
        ),
        cost_estimate=pl.CostEstimate(flops=10**10, bytes_accessed=10**7, transcendentals=10**8),
    )(points, counts.reshape(1, SH), latent.reshape(1, SH), probes)


def solution(mesh):
    spec = ("row", "col", "layer")
    groups = mesh.shape["row"] * 2
    members = mesh.shape["col"] // 2 * mesh.shape["layer"]
    return jax.shard_map(
        functools.partial(local, groups, members),
        mesh=mesh,
        in_specs=(P(None, spec), P(spec), P(spec), P(None, spec)),
        out_specs=P(None, spec),
        check_vma=False,
    )
```

```python
import functools
import math

import jax
import jax.numpy as jnp
from jax import lax
from jax.experimental import pallas as pl
from jax.experimental.pallas import tpu as pltpu
from jax.sharding import PartitionSpec as P

LENGTH = 0.25
AMP = 0.02
DISP = 4.0

MESH = pl.DeviceIdType.MESH
SH = 1024
BI, BJ = 512, 256
TILES = (SH // BI) * (SH // BJ)
WIDE = 2
DEPTH = TILES * WIDE
FEAT = 48

L2E = math.log2(math.e)
COORD = math.sqrt(5.0) / LENGTH * L2E
H = 1.5 * L2E
D = 0.75 * L2E * L2E
B0 = math.log2(AMP / (3.0 * L2E * L2E))
UP = 2.0**-13


def entries(u):
    s = u * lax.rsqrt(u)
    t = s + H
    return ((t * t + D) * jnp.exp2(B0 - s)).astype(jnp.bfloat16)


def pieces(v):
    high = v.astype(jnp.bfloat16).astype(jnp.float32)
    rest = v - high
    mid = rest.astype(jnp.bfloat16).astype(jnp.float32)
    return high, mid, rest - mid


def packed(pts):
    a = (pts - 0.5) * COORD
    at = lax.broadcasted_iota(jnp.int32, a.shape, 0)
    h, m, l = (jnp.where(at < 3, v, 0.0) for v in pieces(a))
    return jnp.concatenate([h + jnp.roll(m, 4, axis=0), l], axis=0).astype(jnp.bfloat16)


def features(packs):
    both = packs.astype(jnp.float32)
    hm, low = both[:8], both[8:]
    mh = jnp.roll(hm, 4, axis=0)
    at = lax.broadcasted_iota(jnp.int32, hm.shape, 0)
    a = jnp.where(at < 3, hm + mh + low, 0.0)
    nh, nm, nl = pieces(jnp.sum(a * a, axis=0, keepdims=True) + UP)
    ones = jnp.where(at < 3, 1.0, 0.0)
    sq = jnp.where(at == 0, nh, jnp.where(at == 1, nm, jnp.where(at == 2, nl, 0.0)))
    left = jnp.concatenate([hm, hm, hm, low, sq, ones], axis=0)
    right = jnp.concatenate([-2.0 * hm, -2.0 * mh, -2.0 * low, -2.0 * hm, ones, sq], axis=0)
    return left, right


def plan(members):
    half = members // 2
    top = members - 1
    low, high = range(half), range(half, members)
    pairs = [(i, j) for j in low for i in low] + [(i, j) for j in low for i in high]
    pairs += [(i, j) for i in low for j in high]
    for k in high:
        pairs += [(k, j) for j in range(top, k - 1, -1)] + [(i, k) for i in range(top, k, -1)]
    outside = [(0, i, 1, j) for i, j in pairs]
    inside = [(side, i, side, j) for side in (0, 1) for j in low for i in range(j)]
    inside += [(side, i, side, j) for side in (0, 1) for i in range(members) for j in range(max(half, i + 1), members)]
    first = len(outside) - len(inside)
    inside = [None] * first + inside

    def uses(cells, shard):
        return [n for n, cell in enumerate(cells) if cell and shard in (cell[:2], cell[2:])]

    shards = [(1, k) for k in range(members)] + [(0, k) for k in range(1, members)]
    take = {shard: uses(outside, shard)[0] - 1 for shard in shards}
    for shard in shards:
        take[shard] = -1 if take[shard] < half - 1 else take[shard]
        assert take[shard] < first or take[shard] < uses(inside, shard)[0]
    send = {k: 2 * (k - half) if k >= half else -1 for k in range(1, members)}
    give = []
    for cells in (outside, inside):
        steps, at = {}, 0
        for last, shard in sorted((uses(cells, shard)[-1], shard) for shard in shards):
            at = max(last + 1, at + 1)
            steps[shard] = at
        give.append(steps)
    return outside, inside, first, take, send, give


def kernel(groups, members, pts_hbm, cnt_hbm, lat_hbm, prb_hbm, out, pts, cnt, lat, prb, xs, fi, fj, sums, parts, own, *rest):
    us, ks = rest[:DEPTH], rest[DEPTH : 2 * DEPTH]
    load, xsend, xrecv, psend, precv = rest[2 * DEPTH :]
    row, col, layer = lax.axis_index("row"), lax.axis_index("col"), lax.axis_index("layer")
    a = row * 2 + lax.rem(col, 2)
    m = lax.div(col, 2) * 2 + layer
    b = lax.rem(a + m + 1, groups)

    def dev(group, member):
        return (lax.div(group, 2), lax.div(member, 2) * 2 + lax.rem(group, 2), lax.rem(member, 2))

    def mate(k):
        return lax.rem(m + k, members)

    def back(k):
        return lax.rem(m + members - k, members)

    asker = dev(lax.rem(a + groups - m - 1, groups), m)

    def cols(j):
        return pl.ds(pl.multiple_of(j * SH, SH), SH)

    pts[...] = jnp.zeros_like(pts)
    loads = [
        pltpu.make_async_copy(src, dst, load.at[n])
        for n, (src, dst) in enumerate([(pts_hbm, pts.at[0:3]), (cnt_hbm, cnt), (lat_hbm, lat), (prb_hbm, prb)])
    ]
    for copy in loads:
        copy.start()
    barrier = pltpu.get_barrier_semaphore()
    pl.semaphore_signal(barrier, inc=1, device_id=dev(b, m), device_id_type=MESH)
    for k in range(1, members):
        pl.semaphore_signal(barrier, inc=1, device_id=dev(a, mate(k)), device_id_type=MESH)

    sums[...] = jnp.zeros_like(sums)
    for k in ks:
        k[...] = jnp.zeros_like(k)
    for copy in loads:
        copy.wait()

    mean_val = jnp.exp(lat[...])
    weight = DISP * mean_val * (DISP + cnt[...].astype(jnp.float32)) / (DISP + mean_val) ** 2
    root = jnp.sqrt(weight)
    xs[0, m, 0:16, :] = (root * prb[...]).astype(jnp.bfloat16)
    xs[0, m, 16:32, :] = packed(pts[...])

    inside = jnp.logical_and(m == members - 1, a >= members)

    def build_left(which, j):
        fi[which, cols(j), :] = features(xs[which, j, 16:32, :])[0].T.astype(jnp.bfloat16)

    def build_right(which, j):
        fj[which, :, cols(j)] = features(xs[which, j, 16:32, :])[1].astype(jnp.bfloat16)

    build_left(0, m)
    build_right(0, m)
    for first in range(0, SH, BI):
        rows = pl.ds(pl.multiple_of(m * SH + first, BI), BI)
        for at in range(first, SH, BJ):
            at_cols = pl.ds(pl.multiple_of(m * SH + at, BJ), BJ)
            k = entries(jnp.dot(fi[0, rows, :], fj[0, :, at_cols], preferred_element_type=jnp.float32))
            term = jnp.dot(xs[0, m, 0:16, first : first + BI], k, preferred_element_type=jnp.float32)
            if first == 0:
                own[:, at : at + BJ] = term
            else:
                own[:, at : at + BJ] += term
            if at >= first + BI:
                own[:, first : first + BI] += lax.dot_general(
                    xs[0, m, 0:16, at : at + BJ], k, (((1,), (1,)), ((), ())), preferred_element_type=jnp.float32
                )

    pl.semaphore_wait(barrier, members)

    def remote(src, dst, ssem, rsem, to):
        return pltpu.make_async_remote_copy(
            src_ref=src, dst_ref=dst, send_sem=ssem, recv_sem=rsem, device_id=to, device_id_type=MESH
        )

    def ask(k):
        j = mate(k)
        return remote(xs.at[0, j], xs.at[1, j], xsend.at[k], xrecv.at[1, j], asker)

    def share(k):
        return remote(xs.at[0, m], xs.at[0, m], xsend.at[members - 1 + k], xrecv.at[0, m], dev(a, back(k)))

    outside_cells, inside_cells, first_inside, take_at, send_at, give_at = plan(members)
    steps = len(outside_cells)

    ask(0).start()
    for k, n in send_at.items():
        if n < 0:
            share(k).start()

    def arrived(ref, sem):
        remote(ref, ref, psend.at[0], sem, dev(a, mate(1))).wait_recv()

    def take_first(k):
        j = mate(k)
        arrived(xs.at[0, j], xrecv.at[0, j])
        ask(k).start()
        build_left(0, j)

        @pl.when(inside)
        def _():
            build_right(0, j)

    def take_second(k):
        j = mate(k)
        arrived(xs.at[1, j], xrecv.at[1, j])
        build_right(1, j)

        @pl.when(inside)
        def _():
            build_left(1, j)

    start = jnp.where(inside, first_inside, 0)

    def look(at, table):
        found = jnp.int32(0)
        for n, value in table.items():
            found = jnp.where(at == n, value, found)
        return found

    def code(which, k):
        return which * members + k

    cells = {}
    for kind, listed in enumerate((outside_cells, inside_cells)):
        for n, at in enumerate(listed):
            if at is not None:
                cells[n + kind * steps] = code(*at[:2]) * 2 * members + code(*at[2:])

    def shard_of(value):
        which = lax.div(value, members)
        k = lax.rem(value, members)
        return which, mate(k)

    kind_at = jnp.where(inside, steps, 0)

    def cell(c):
        return look(jnp.minimum(c, steps - 1) + kind_at, cells)

    def place(at, n):
        si, i = shard_of(lax.div(at, 2 * members))
        sj, j = shard_of(lax.rem(at, 2 * members))
        first, second = (n % (SH // BI)) * BI, (n % TILES // (SH // BI)) * BJ
        rows = pl.ds(pl.multiple_of(i * SH + first, BI), BI)
        at_cols = pl.ds(pl.multiple_of(j * SH + second, BJ), BJ)
        return si, rows, sj, at_cols, xs.at[si, i, 0:16, first : first + BI], xs.at[sj, j, 0:16, second : second + BJ]

    def distance(at, n, u):
        si, rows, sj, at_cols, _, _ = place(at, n)
        u[...] = jnp.dot(fi[si, rows, :], fj[sj, :, at_cols], preferred_element_type=jnp.float32)

    def products(at, n, k):
        si, rows, sj, at_cols, ci, cj = place(at, n)
        kv = k[...]
        sums[sj, :, at_cols] += jnp.dot(ci[...], kv, preferred_element_type=jnp.float32)
        sums[si, :, rows] += lax.dot_general(
            cj[...], kv, (((1,), (1,)), ((), ())), preferred_element_type=jnp.float32
        )

    def give_row(k):
        j = mate(k)
        return remote(sums.at[0, :, cols(j)], parts.at[m], psend.at[k - 1], precv.at[m], dev(a, j))

    def give_col(k):
        j = mate(k)
        return remote(sums.at[1, :, cols(j)], parts.at[members + m], psend.at[members - 1 + k], precv.at[members + m], dev(b, j))

    sending = {n: k for k, n in send_at.items() if n >= 0}
    taking = {n: code(*shard) + 1 for shard, n in take_at.items() if n >= 0}
    giving, after_loop = {}, []
    for kind, table in enumerate(give_at):
        for shard, n in table.items():
            if n + 1 <= steps - WIDE:
                giving[n + 1 + kind * steps] = code(*shard) + 1
            else:
                after_loop.append((n, kind, shard))

    def fetch_events(c):
        return [(look(c + n, sending), look(c + n, taking)) for n in range(WIDE)]

    def give_events(c):
        return [look(c - n + kind_at, giving) for n in range(WIDE)]

    def fetch(events):
        for send, arrival in events:

            @pl.when(send > 0)
            def _(send=send):
                share(send).start()

            @pl.when(arrival > members)
            def _(arrival=arrival):
                take_second(arrival - 1 - members)

            @pl.when(jnp.logical_and(arrival > 0, arrival <= members))
            def _(arrival=arrival):
                take_first(arrival - 1)

    def give(events):
        for shard in events:

            @pl.when(shard > members)
            def _(shard=shard):
                give_col(shard - 1 - members).start()

            @pl.when(jnp.logical_and(shard > 0, shard <= members))
            def _(shard=shard):
                give_row(shard - 1).start()

    for (which, k), n in sorted(take_at.items()):
        if n < 0 and which == 0:
            take_first(k)
    take_second(0)

    def early(p, carry):
        fetch(fetch_events(p * WIDE))
        return carry

    lax.fori_loop(0, lax.div(start, WIDE), early, 0)
    begin = cell(start)
    distance(begin, 0, us[0])

    def step(p, carry):
        last, this, events, given = carry
        any_event = sum(given)
        for send, arrival in events:
            any_event = any_event + send + arrival

        @pl.when(any_event > 0)
        def _():
            give(given)
            fetch(events)

        c = p * WIDE
        held = [this, *[cell(c + n) for n in range(1, WIDE + 1)]]
        for n in range(DEPTH):
            distance(held[(n + 1) // TILES], n + 1, us[(n + 1) % DEPTH])
            products(held[(n - 1) // TILES] if n else last, n - 1, ks[(n - 1) % DEPTH])
            ks[n][...] = entries(us[n][...])
        return held[-2], held[-1], fetch_events(c + WIDE), give_events(c + WIDE)

    carry = (begin, begin, fetch_events(start), give_events(start))
    last, *_ = lax.fori_loop(lax.div(start, WIDE), steps // WIDE, step, carry)
    products(last, DEPTH - 1, ks[DEPTH - 1])
    for n, kind, (which, k) in sorted(after_loop):

        @pl.when(inside if kind else jnp.logical_not(inside))
        def _(which=which, k=k):
            (give_col if which else give_row)(k).start()

    total = own[...] + sums[0, :, cols(m)]
    for k in range(members):
        arrived(parts.at[members + k], precv.at[members + k])
        total = total + parts[members + k]
        if k:
            arrived(parts.at[mate(k)], precv.at[mate(k)])
            total = total + parts[mate(k)]
    out[...] = prb[...] + root * total
    for k in range(members):
        ask(k).wait_send()
        give_col(k).wait_send()
        if k:
            share(k).wait_send()
            give_row(k).wait_send()


def local(groups, members, points, counts, latent, probes):
    size = members * SH
    copies = 2 * members - 1
    return pl.pallas_call(
        functools.partial(kernel, groups, members),
        out_shape=jax.ShapeDtypeStruct(probes.shape, jnp.float32),
        in_specs=[pl.BlockSpec(memory_space=pl.ANY)] * 4,
        out_specs=pl.BlockSpec(memory_space=pltpu.VMEM),
        scratch_shapes=[
            pltpu.VMEM((8, SH), jnp.float32),
            pltpu.VMEM((1, SH), jnp.int32),
            pltpu.VMEM((1, SH), jnp.float32),
            pltpu.VMEM((16, SH), jnp.float32),
            pltpu.VMEM((2, members, 32, SH), jnp.bfloat16),
            pltpu.VMEM((2, size, FEAT), jnp.bfloat16),
            pltpu.VMEM((2, FEAT, size), jnp.bfloat16),
            pltpu.VMEM((2, 16, size), jnp.float32),
            pltpu.VMEM((2 * members, 16, SH), jnp.float32),
            pltpu.VMEM((16, SH), jnp.float32),
            *[pltpu.VMEM((BI, BJ), jnp.float32)] * DEPTH,
            *[pltpu.VMEM((BI, BJ), jnp.bfloat16)] * DEPTH,
            pltpu.SemaphoreType.DMA((4,)),
            pltpu.SemaphoreType.DMA((copies,)),
            pltpu.SemaphoreType.DMA((2, members)),
            pltpu.SemaphoreType.DMA((copies,)),
            pltpu.SemaphoreType.DMA((2 * members,)),
        ],
        compiler_params=pltpu.CompilerParams(
            collective_id=0, has_side_effects=True, vmem_limit_bytes=60 * 2**20
        ),
        cost_estimate=pl.CostEstimate(flops=10**10, bytes_accessed=10**7, transcendentals=10**8),
    )(points, counts.reshape(1, SH), latent.reshape(1, SH), probes)


def solution(mesh):
    spec = ("row", "col", "layer")
    groups = mesh.shape["row"] * 2
    members = mesh.shape["col"] // 2 * mesh.shape["layer"]
    return jax.shard_map(
        functools.partial(local, groups, members),
        mesh=mesh,
        in_specs=(P(None, spec), P(spec), P(spec), P(None, spec)),
        out_specs=P(None, spec),
        check_vma=False,
    )
```

```python
import functools
import math

import jax
import jax.numpy as jnp
from jax import lax
from jax.experimental import pallas as pl
from jax.experimental.pallas import tpu as pltpu
from jax.sharding import PartitionSpec as P

LENGTH = 0.25
AMP = 0.02
DISP = 4.0

MESH = pl.DeviceIdType.MESH
SH = 1024
BI, BJ = 256, 256
TILES = (SH // BI) * (SH // BJ)
WIDE = 2
DEPTH = TILES * WIDE
FEAT = 48

L2E = math.log2(math.e)
COORD = math.sqrt(5.0) / LENGTH * L2E
H = 1.5 * L2E
C = 3.0 * L2E * L2E
B0 = math.log2(AMP / (3.0 * L2E * L2E))
UP = 2.0**-13


def entries(square, more):
    s = square * lax.rsqrt(square)
    return ((more + (2.0 * H) * s) * jnp.exp2(B0 - s)).astype(jnp.bfloat16)


def pieces(v):
    high = v.astype(jnp.bfloat16).astype(jnp.float32)
    rest = v - high
    mid = rest.astype(jnp.bfloat16).astype(jnp.float32)
    return high, mid, rest - mid


def packed(pts):
    a = (pts - 0.5) * COORD
    at = lax.broadcasted_iota(jnp.int32, a.shape, 0)
    h, m, l = (jnp.where(at < 3, v, 0.0) for v in pieces(a))
    return jnp.concatenate([h + jnp.roll(m, 4, axis=0), l], axis=0).astype(jnp.bfloat16)


def features(packs):
    both = packs.astype(jnp.float32)
    hm, low = both[:8], both[8:]
    mh = jnp.roll(hm, 4, axis=0)
    at = lax.broadcasted_iota(jnp.int32, hm.shape, 0)
    a = jnp.where(at < 3, hm + mh + low, 0.0)
    norm = jnp.sum(a * a, axis=0, keepdims=True) + UP
    ones = jnp.where(at < 3, 1.0, 0.0)

    def rows(v):
        high, mid, low = pieces(v)
        return jnp.where(at == 0, high, jnp.where(at == 1, mid, jnp.where(at == 2, low, 0.0)))

    left = jnp.concatenate([hm, hm, hm, low, rows(norm), ones], axis=0)
    right = [-2.0 * hm, -2.0 * mh, -2.0 * low, -2.0 * hm, ones]
    return left, jnp.concatenate([*right, rows(norm), *right, rows(norm + C)], axis=0)


def plan(members):
    own_last = [*range(1, members), 0]
    pairs = [(i, j) for j in range(members) for i in (own_last if j == members - 1 else range(members))]
    outside = [(0, i, 1, j) for i, j in pairs]
    inside = [(side, i, side, j) for side in (0, 1) for j in range(members) for i in range(j)]
    first = len(outside) - len(inside)
    inside = [None] * first + inside

    def uses(cells, shard):
        return [n for n, cell in enumerate(cells) if cell and shard in (cell[:2], cell[2:])]

    shards = [(1, k) for k in range(members)] + [(0, k) for k in range(1, members)]
    take = {shard: uses(outside, shard)[0] - 1 for shard in shards}
    for shard in shards:
        take[shard] = -1 if take[shard] <= 2 else take[shard]
        assert take[shard] < first or take[shard] < uses(inside, shard)[0]
    send = {k: k - 6 if k >= 6 else -1 for k in range(1, members)}
    give = []
    for cells in (outside, inside):
        steps, at = {}, 0
        for last, shard in sorted((uses(cells, shard)[-1], shard) for shard in shards):
            at = max(last + 1, at + 1)
            steps[shard] = at
        give.append(steps)
    return outside, inside, first, take, send, give


def kernel(groups, members, pts_hbm, cnt_hbm, lat_hbm, prb_hbm, out, pts, cnt, lat, prb, xs, fi, fj, sums, parts, own, *rest):
    us, vs, ks = rest[:DEPTH], rest[DEPTH : 2 * DEPTH], rest[2 * DEPTH : 3 * DEPTH]
    load, xsend, xrecv, psend, precv = rest[3 * DEPTH :]
    row, col, layer = lax.axis_index("row"), lax.axis_index("col"), lax.axis_index("layer")
    a = row * 2 + lax.rem(col, 2)
    m = lax.div(col, 2) * 2 + layer
    b = lax.rem(a + m + 1, groups)

    def dev(group, member):
        return (lax.div(group, 2), lax.div(member, 2) * 2 + lax.rem(group, 2), lax.rem(member, 2))

    def mate(k):
        return lax.rem(m + k, members)

    def back(k):
        return lax.rem(m + members - k, members)

    asker = dev(lax.rem(a + groups - m - 1, groups), m)

    def cols(j):
        return pl.ds(pl.multiple_of(j * SH, SH), SH)

    barrier = pltpu.get_barrier_semaphore()
    pl.semaphore_signal(barrier, inc=1, device_id=dev(b, m), device_id_type=MESH)
    for k in range(1, members):
        pl.semaphore_signal(barrier, inc=1, device_id=dev(a, mate(k)), device_id_type=MESH)

    pts[...] = jnp.zeros_like(pts)
    loads = [
        pltpu.make_async_copy(src, dst, load.at[n])
        for n, (src, dst) in enumerate([(pts_hbm, pts.at[0:3]), (cnt_hbm, cnt), (lat_hbm, lat), (prb_hbm, prb)])
    ]
    for copy in loads:
        copy.start()
    sums[...] = jnp.zeros_like(sums)
    for k in ks:
        k[...] = jnp.zeros_like(k)
    for copy in loads:
        copy.wait()

    mean_val = jnp.exp(lat[...])
    weight = DISP * mean_val * (DISP + cnt[...].astype(jnp.float32)) / (DISP + mean_val) ** 2
    root = jnp.sqrt(weight)
    xs[0, m, 0:16, :] = (root * prb[...]).astype(jnp.bfloat16)
    xs[0, m, 16:32, :] = packed(pts[...])

    inside = jnp.logical_and(m == members - 1, a >= members)

    def build_left(which, j):
        fi[which, cols(j), :] = features(xs[which, j, 16:32, :])[0].T.astype(jnp.bfloat16)

    def build_right(which, j):
        fj[which, :, cols(j)] = features(xs[which, j, 16:32, :])[1].astype(jnp.bfloat16)

    def squares(si, rows, sj, at_cols):
        left = fi[si, rows, :]
        return [
            jnp.dot(left, fj[sj, n * FEAT : (n + 1) * FEAT, at_cols], preferred_element_type=jnp.float32)
            for n in range(2)
        ]

    build_left(0, m)
    build_right(0, m)
    for first in range(0, SH, BI):
        rows = pl.ds(pl.multiple_of(m * SH + first, BI), BI)
        for at in range(first, SH, BJ):
            at_cols = pl.ds(pl.multiple_of(m * SH + at, BJ), BJ)
            k = entries(*squares(0, rows, 0, at_cols))
            term = jnp.dot(xs[0, m, 0:16, first : first + BI], k, preferred_element_type=jnp.float32)
            if first == 0:
                own[:, at : at + BJ] = term
            else:
                own[:, at : at + BJ] += term
            if at >= first + BI:
                own[:, first : first + BI] += lax.dot_general(
                    xs[0, m, 0:16, at : at + BJ], k, (((1,), (1,)), ((), ())), preferred_element_type=jnp.float32
                )

    pl.semaphore_wait(barrier, members)

    def remote(src, dst, ssem, rsem, to):
        return pltpu.make_async_remote_copy(
            src_ref=src, dst_ref=dst, send_sem=ssem, recv_sem=rsem, device_id=to, device_id_type=MESH
        )

    def ask(k):
        j = mate(k)
        return remote(xs.at[0, j], xs.at[1, j], xsend.at[k], xrecv.at[1, j], asker)

    def share(k):
        return remote(xs.at[0, m], xs.at[0, m], xsend.at[members - 1 + k], xrecv.at[0, m], dev(a, back(k)))

    outside_cells, inside_cells, first_inside, take_at, send_at, give_at = plan(members)
    steps = len(outside_cells)

    ask(0).start()
    for k, n in send_at.items():
        if n < 0:
            share(k).start()

    def arrived(ref, sem):
        remote(ref, ref, psend.at[0], sem, dev(a, mate(1))).wait_recv()

    def take_first(k):
        j = mate(k)
        arrived(xs.at[0, j], xrecv.at[0, j])
        ask(k).start()
        build_left(0, j)

        @pl.when(inside)
        def _():
            build_right(0, j)

    def take_second(k):
        j = mate(k)
        arrived(xs.at[1, j], xrecv.at[1, j])
        build_right(1, j)

        @pl.when(inside)
        def _():
            build_left(1, j)

    start = jnp.where(inside, first_inside, 0)

    def look(at, table):
        found = jnp.int32(0)
        for n, value in table.items():
            found = jnp.where(at == n, value, found)
        return found

    def code(which, k):
        return which * members + k

    cells = {}
    for kind, listed in enumerate((outside_cells, inside_cells)):
        for n, at in enumerate(listed):
            if at is not None:
                cells[n + kind * steps] = code(*at[:2]) * 2 * members + code(*at[2:])

    def shard_of(value):
        which = lax.div(value, members)
        k = lax.rem(value, members)
        return which, mate(k)

    kind_at = jnp.where(inside, steps, 0)

    def cell(c):
        return look(jnp.minimum(c, steps - 1) + kind_at, cells)

    def place(at, n):
        si, i = shard_of(lax.div(at, 2 * members))
        sj, j = shard_of(lax.rem(at, 2 * members))
        first, second = (n % (SH // BI)) * BI, (n % TILES // (SH // BI)) * BJ
        rows = pl.ds(pl.multiple_of(i * SH + first, BI), BI)
        at_cols = pl.ds(pl.multiple_of(j * SH + second, BJ), BJ)
        return si, rows, sj, at_cols, xs.at[si, i, 0:16, first : first + BI], xs.at[sj, j, 0:16, second : second + BJ]

    def distance(at, n):
        si, rows, sj, at_cols, _, _ = place(at, n)
        n = n % DEPTH
        us[n][...], vs[n][...] = squares(si, rows, sj, at_cols)

    def products(at, n, k):
        si, rows, sj, at_cols, ci, cj = place(at, n)
        kv = k[...]
        sums[sj, :, at_cols] += jnp.dot(ci[...], kv, preferred_element_type=jnp.float32)
        sums[si, :, rows] += lax.dot_general(
            cj[...], kv, (((1,), (1,)), ((), ())), preferred_element_type=jnp.float32
        )

    def give_row(k):
        j = mate(k)
        return remote(sums.at[0, :, cols(j)], parts.at[m], psend.at[k - 1], precv.at[m], dev(a, j))

    def give_col(k):
        j = mate(k)
        return remote(sums.at[1, :, cols(j)], parts.at[members + m], psend.at[members - 1 + k], precv.at[members + m], dev(b, j))

    sending = {n: k for k, n in send_at.items() if n >= 0}
    taking = {n: code(*shard) + 1 for shard, n in take_at.items() if n >= 0}
    giving, after_loop = {}, []
    for kind, table in enumerate(give_at):
        for shard, n in table.items():
            if n + 1 <= steps - WIDE:
                giving[n + 1 + kind * steps] = code(*shard) + 1
            else:
                after_loop.append((n, kind, shard))

    def fetch_events(c):
        return [(look(c + n, sending), look(c + n, taking)) for n in range(WIDE)]

    def give_events(c):
        return [look(c - n + kind_at, giving) for n in range(WIDE)]

    def fetch(events):
        for send, arrival in events:

            @pl.when(send > 0)
            def _(send=send):
                share(send).start()

            @pl.when(arrival > members)
            def _(arrival=arrival):
                take_second(arrival - 1 - members)

            @pl.when(jnp.logical_and(arrival > 0, arrival <= members))
            def _(arrival=arrival):
                take_first(arrival - 1)

    def give(events):
        for shard in events:

            @pl.when(shard > members)
            def _(shard=shard):
                give_col(shard - 1 - members).start()

            @pl.when(jnp.logical_and(shard > 0, shard <= members))
            def _(shard=shard):
                give_row(shard - 1).start()

    for (which, k), n in sorted(take_at.items()):
        if n < 0 and which == 0:
            take_first(k)
    take_second(0)

    def early(p, carry):
        fetch(fetch_events(p * WIDE))
        return carry

    lax.fori_loop(0, lax.div(start, WIDE), early, 0)
    begin = cell(start)
    distance(begin, 0)

    def step(p, carry):
        last, this, events, given = carry
        any_event = sum(given)
        for send, arrival in events:
            any_event = any_event + send + arrival

        @pl.when(any_event > 0)
        def _():
            give(given)
            fetch(events)

        c = p * WIDE
        held = [this, *[cell(c + n) for n in range(1, WIDE + 1)]]
        for n in range(DEPTH):
            distance(held[(n + 1) // TILES], n + 1)
            products(held[(n - 1) // TILES] if n else last, n - 1, ks[(n - 1) % DEPTH])
            ks[n][...] = entries(us[n][...], vs[n][...])
        return held[-2], held[-1], fetch_events(c + WIDE), give_events(c + WIDE)

    carry = (begin, begin, fetch_events(start), give_events(start))
    last, *_ = lax.fori_loop(lax.div(start, WIDE), steps // WIDE, step, carry)
    products(last, DEPTH - 1, ks[DEPTH - 1])
    for n, kind, (which, k) in sorted(after_loop, key=lambda late: (-late[2][0], late[0])):

        @pl.when(inside if kind else jnp.logical_not(inside))
        def _(which=which, k=k):
            (give_col if which else give_row)(k).start()

    total = own[...] + sums[0, :, cols(m)]
    for k in range(members):
        arrived(parts.at[members + k], precv.at[members + k])
        total = total + parts[members + k]
        if k:
            arrived(parts.at[mate(k)], precv.at[mate(k)])
            total = total + parts[mate(k)]
    out[...] = prb[...] + root * total
    for k in range(members):
        ask(k).wait_send()
        give_col(k).wait_send()
        if k:
            share(k).wait_send()
            give_row(k).wait_send()


def local(groups, members, points, counts, latent, probes):
    size = members * SH
    copies = 2 * members - 1
    return pl.pallas_call(
        functools.partial(kernel, groups, members),
        out_shape=jax.ShapeDtypeStruct(probes.shape, jnp.float32),
        in_specs=[pl.BlockSpec(memory_space=pl.ANY)] * 4,
        out_specs=pl.BlockSpec(memory_space=pltpu.VMEM),
        scratch_shapes=[
            pltpu.VMEM((8, SH), jnp.float32),
            pltpu.VMEM((1, SH), jnp.int32),
            pltpu.VMEM((1, SH), jnp.float32),
            pltpu.VMEM((16, SH), jnp.float32),
            pltpu.VMEM((2, members, 32, SH), jnp.bfloat16),
            pltpu.VMEM((2, size, FEAT), jnp.bfloat16),
            pltpu.VMEM((2, 2 * FEAT, size), jnp.bfloat16),
            pltpu.VMEM((2, 16, size), jnp.float32),
            pltpu.VMEM((2 * members, 16, SH), jnp.float32),
            pltpu.VMEM((16, SH), jnp.float32),
            *[pltpu.VMEM((BI, BJ), jnp.float32)] * (2 * DEPTH),
            *[pltpu.VMEM((BI, BJ), jnp.bfloat16)] * DEPTH,
            pltpu.SemaphoreType.DMA((4,)),
            pltpu.SemaphoreType.DMA((copies,)),
            pltpu.SemaphoreType.DMA((2, members)),
            pltpu.SemaphoreType.DMA((copies,)),
            pltpu.SemaphoreType.DMA((2 * members,)),
        ],
        compiler_params=pltpu.CompilerParams(
            collective_id=0, has_side_effects=True, vmem_limit_bytes=60 * 2**20
        ),
        cost_estimate=pl.CostEstimate(flops=10**10, bytes_accessed=10**7, transcendentals=10**8),
    )(points, counts.reshape(1, SH), latent.reshape(1, SH), probes)


def solution(mesh):
    spec = ("row", "col", "layer")
    groups = mesh.shape["row"] * 2
    members = mesh.shape["col"] // 2 * mesh.shape["layer"]
    return jax.shard_map(
        functools.partial(local, groups, members),
        mesh=mesh,
        in_specs=(P(None, spec), P(spec), P(spec), P(None, spec)),
        out_specs=P(None, spec),
        check_vma=False,
    )
```

```python
import functools
import math

import jax
import jax.numpy as jnp
from jax import lax
from jax.experimental import pallas as pl
from jax.experimental.pallas import tpu as pltpu
from jax.sharding import PartitionSpec as P

LENGTH = 0.25
AMP = 0.02
DISP = 4.0

MESH = pl.DeviceIdType.MESH
SH = 1024
BI, BJ = 256, 256
TILES = (SH // BI) * (SH // BJ)
WIDE = 2
DEPTH = TILES * WIDE
FEAT = 32

L2E = math.log2(math.e)
COORD = math.sqrt(5.0) / LENGTH * L2E
H = 1.5 * L2E
C = 3.0 * L2E * L2E
B0 = math.log2(AMP / (3.0 * L2E * L2E))
UP = 2.0**-13


def entries(square, more):
    s = square * lax.rsqrt(square)
    return ((more + (2.0 * H) * s) * jnp.exp2(B0 - s)).astype(jnp.bfloat16)


def pieces(v):
    high = v.astype(jnp.bfloat16).astype(jnp.float32)
    rest = v - high
    mid = rest.astype(jnp.bfloat16).astype(jnp.float32)
    return high, mid, rest - mid


def packed(pts):
    a = (pts - 0.5) * COORD
    at = lax.broadcasted_iota(jnp.int32, a.shape, 0)
    h, m, l = (jnp.where(at < 3, v, 0.0) for v in pieces(a))
    return jnp.concatenate([h + jnp.roll(m, 4, axis=0), l], axis=0).astype(jnp.bfloat16)


def features(packs):
    both = packs.astype(jnp.float32)
    hm, low = both[:8], both[8:]
    mh = jnp.roll(hm, 4, axis=0)
    at = lax.broadcasted_iota(jnp.int32, hm.shape, 0)
    a = jnp.where(at < 3, hm + mh + low, 0.0)
    norm = jnp.sum(a * a, axis=0, keepdims=True) + UP
    ones = jnp.where(at < 3, 1.0, 0.0)

    def rows(v):
        high, mid, low = pieces(v)
        return jnp.where(at == 0, high, jnp.where(at == 1, mid, jnp.where(at == 2, low, 0.0)))

    def other(v):
        return jnp.roll(v, 4, axis=0)

    hl = jnp.where(at < 3, hm, other(low))
    left = jnp.concatenate([hm, hm, hl, rows(norm) + other(ones)], axis=0)
    right = [-2.0 * hm, -2.0 * mh, -2.0 * other(hl)]
    return left, jnp.concatenate([*right, ones + other(rows(norm)), *right, ones + other(rows(norm + C))], axis=0)


def plan(members):
    own_last = [*range(1, members), 0]
    pairs = [(i, j) for j in range(members) for i in (own_last if j == members - 1 else range(members))]
    outside = [(0, i, 1, j) for i, j in pairs]
    inside = [(side, i, side, j) for side in (0, 1) for j in range(members) for i in range(j)]
    first = len(outside) - len(inside)
    inside = [None] * first + inside

    def uses(cells, shard):
        return [n for n, cell in enumerate(cells) if cell and shard in (cell[:2], cell[2:])]

    shards = [(1, k) for k in range(members)] + [(0, k) for k in range(1, members)]
    take = {shard: uses(outside, shard)[0] - 1 for shard in shards}
    for shard in shards:
        take[shard] = -1 if take[shard] <= 2 else take[shard]
        assert take[shard] < first or take[shard] < uses(inside, shard)[0]
    send = {k: k - 6 if k >= 6 else -1 for k in range(1, members)}
    give = []
    for cells in (outside, inside):
        steps, at = {}, 0
        for last, shard in sorted((uses(cells, shard)[-1], shard) for shard in shards):
            at = max(last + 1, at + 1)
            steps[shard] = at
        give.append(steps)
    return outside, inside, first, take, send, give


def kernel(groups, members, pts_hbm, cnt_hbm, lat_hbm, prb_hbm, out, pts, cnt, lat, prb, xs, fi, fj, sums, parts, own, *rest):
    us, vs, ks = rest[:DEPTH], rest[DEPTH : 2 * DEPTH], rest[2 * DEPTH : 3 * DEPTH]
    load, xsend, xrecv, psend, precv = rest[3 * DEPTH :]
    row, col, layer = lax.axis_index("row"), lax.axis_index("col"), lax.axis_index("layer")
    a = row * 2 + lax.rem(col, 2)
    m = lax.div(col, 2) * 2 + layer
    b = lax.rem(a + m + 1, groups)

    def dev(group, member):
        return (lax.div(group, 2), lax.div(member, 2) * 2 + lax.rem(group, 2), lax.rem(member, 2))

    def mate(k):
        return lax.rem(m + k, members)

    def back(k):
        return lax.rem(m + members - k, members)

    asker = dev(lax.rem(a + groups - m - 1, groups), m)

    def cols(j):
        return pl.ds(pl.multiple_of(j * SH, SH), SH)

    barrier = pltpu.get_barrier_semaphore()
    pl.semaphore_signal(barrier, inc=1, device_id=dev(b, m), device_id_type=MESH)
    for k in range(1, members):
        pl.semaphore_signal(barrier, inc=1, device_id=dev(a, mate(k)), device_id_type=MESH)

    pts[...] = jnp.zeros_like(pts)
    loads = [
        pltpu.make_async_copy(src, dst, load.at[n])
        for n, (src, dst) in enumerate([(pts_hbm, pts.at[0:3]), (cnt_hbm, cnt), (lat_hbm, lat), (prb_hbm, prb)])
    ]
    for copy in loads:
        copy.start()
    sums[...] = jnp.zeros_like(sums)
    for k in ks:
        k[...] = jnp.zeros_like(k)
    for copy in loads:
        copy.wait()

    mean_val = jnp.exp(lat[...])
    weight = DISP * mean_val * (DISP + cnt[...].astype(jnp.float32)) / (DISP + mean_val) ** 2
    root = jnp.sqrt(weight)
    xs[0, m, 0:16, :] = (root * prb[...]).astype(jnp.bfloat16)
    xs[0, m, 16:32, :] = packed(pts[...])

    inside = jnp.logical_and(m == members - 1, a >= members)

    def build_left(which, j):
        fi[which, cols(j), :] = features(xs[which, j, 16:32, :])[0].T.astype(jnp.bfloat16)

    def build_right(which, j):
        fj[which, :, cols(j)] = features(xs[which, j, 16:32, :])[1].astype(jnp.bfloat16)

    def squares(si, rows, sj, at_cols):
        left = fi[si, rows, :]
        return [
            jnp.dot(left, fj[sj, n * FEAT : (n + 1) * FEAT, at_cols], preferred_element_type=jnp.float32)
            for n in range(2)
        ]

    build_left(0, m)
    build_right(0, m)
    for first in range(0, SH, BI):
        rows = pl.ds(pl.multiple_of(m * SH + first, BI), BI)
        for at in range(first, SH, BJ):
            at_cols = pl.ds(pl.multiple_of(m * SH + at, BJ), BJ)
            k = entries(*squares(0, rows, 0, at_cols))
            term = jnp.dot(xs[0, m, 0:16, first : first + BI], k, preferred_element_type=jnp.float32)
            if first == 0:
                own[:, at : at + BJ] = term
            else:
                own[:, at : at + BJ] += term
            if at >= first + BI:
                own[:, first : first + BI] += lax.dot_general(
                    xs[0, m, 0:16, at : at + BJ], k, (((1,), (1,)), ((), ())), preferred_element_type=jnp.float32
                )

    pl.semaphore_wait(barrier, members)

    def remote(src, dst, ssem, rsem, to):
        return pltpu.make_async_remote_copy(
            src_ref=src, dst_ref=dst, send_sem=ssem, recv_sem=rsem, device_id=to, device_id_type=MESH
        )

    def ask(k):
        j = mate(k)
        return remote(xs.at[0, j], xs.at[1, j], xsend.at[k], xrecv.at[1, j], asker)

    def share(k):
        return remote(xs.at[0, m], xs.at[0, m], xsend.at[members - 1 + k], xrecv.at[0, m], dev(a, back(k)))

    outside_cells, inside_cells, first_inside, take_at, send_at, give_at = plan(members)
    steps = len(outside_cells)

    ask(0).start()
    for k, n in send_at.items():
        if n < 0:
            share(k).start()

    def arrived(ref, sem):
        remote(ref, ref, psend.at[0], sem, dev(a, mate(1))).wait_recv()

    def take_first(k):
        j = mate(k)
        arrived(xs.at[0, j], xrecv.at[0, j])
        ask(k).start()
        build_left(0, j)

        @pl.when(inside)
        def _():
            build_right(0, j)

    def take_second(k):
        j = mate(k)
        arrived(xs.at[1, j], xrecv.at[1, j])
        build_right(1, j)

        @pl.when(inside)
        def _():
            build_left(1, j)

    start = jnp.where(inside, first_inside, 0)

    def look(at, table):
        found = jnp.int32(0)
        for n, value in table.items():
            found = jnp.where(at == n, value, found)
        return found

    def code(which, k):
        return which * members + k

    cells = {}
    for kind, listed in enumerate((outside_cells, inside_cells)):
        for n, at in enumerate(listed):
            if at is not None:
                cells[n + kind * steps] = code(*at[:2]) * 2 * members + code(*at[2:])

    def shard_of(value):
        which = lax.div(value, members)
        k = lax.rem(value, members)
        return which, mate(k)

    kind_at = jnp.where(inside, steps, 0)

    def cell(c):
        return look(jnp.minimum(c, steps - 1) + kind_at, cells)

    def place(at, n):
        si, i = shard_of(lax.div(at, 2 * members))
        sj, j = shard_of(lax.rem(at, 2 * members))
        first, second = (n % (SH // BI)) * BI, (n % TILES // (SH // BI)) * BJ
        rows = pl.ds(pl.multiple_of(i * SH + first, BI), BI)
        at_cols = pl.ds(pl.multiple_of(j * SH + second, BJ), BJ)
        return si, rows, sj, at_cols, xs.at[si, i, 0:16, first : first + BI], xs.at[sj, j, 0:16, second : second + BJ]

    def distance(at, n):
        si, rows, sj, at_cols, _, _ = place(at, n)
        n = n % DEPTH
        us[n][...], vs[n][...] = squares(si, rows, sj, at_cols)

    def products(at, n, k):
        si, rows, sj, at_cols, ci, cj = place(at, n)
        kv = k[...]
        sums[sj, :, at_cols] += jnp.dot(ci[...], kv, preferred_element_type=jnp.float32)
        sums[si, :, rows] += lax.dot_general(
            cj[...], kv, (((1,), (1,)), ((), ())), preferred_element_type=jnp.float32
        )

    def give_row(k):
        j = mate(k)
        return remote(sums.at[0, :, cols(j)], parts.at[m], psend.at[k - 1], precv.at[m], dev(a, j))

    def give_col(k):
        j = mate(k)
        return remote(sums.at[1, :, cols(j)], parts.at[members + m], psend.at[members - 1 + k], precv.at[members + m], dev(b, j))

    sending = {n: k for k, n in send_at.items() if n >= 0}
    taking = {n: code(*shard) + 1 for shard, n in take_at.items() if n >= 0}
    giving, after_loop = {}, []
    for kind, table in enumerate(give_at):
        for shard, n in table.items():
            if n + 1 <= steps - WIDE:
                giving[n + 1 + kind * steps] = code(*shard) + 1
            else:
                after_loop.append((n, kind, shard))

    def fetch_events(c):
        return [(look(c + n, sending), look(c + n, taking)) for n in range(WIDE)]

    def give_events(c):
        return [look(c - n + kind_at, giving) for n in range(WIDE)]

    def fetch(events):
        for send, arrival in events:

            @pl.when(send > 0)
            def _(send=send):
                share(send).start()

            @pl.when(arrival > members)
            def _(arrival=arrival):
                take_second(arrival - 1 - members)

            @pl.when(jnp.logical_and(arrival > 0, arrival <= members))
            def _(arrival=arrival):
                take_first(arrival - 1)

    def give(events):
        for shard in events:

            @pl.when(shard > members)
            def _(shard=shard):
                give_col(shard - 1 - members).start()

            @pl.when(jnp.logical_and(shard > 0, shard <= members))
            def _(shard=shard):
                give_row(shard - 1).start()

    for (which, k), n in sorted(take_at.items()):
        if n < 0 and which == 0:
            take_first(k)
    take_second(0)

    def early(p, carry):
        fetch(fetch_events(p * WIDE))
        return carry

    lax.fori_loop(0, lax.div(start, WIDE), early, 0)
    begin = cell(start)
    distance(begin, 0)

    def step(p, carry):
        last, this, events, given = carry
        any_event = sum(given)
        for send, arrival in events:
            any_event = any_event + send + arrival

        @pl.when(any_event > 0)
        def _():
            give(given)
            fetch(events)

        c = p * WIDE
        held = [this, *[cell(c + n) for n in range(1, WIDE + 1)]]
        for n in range(DEPTH):
            distance(held[(n + 1) // TILES], n + 1)
            products(held[(n - 1) // TILES] if n else last, n - 1, ks[(n - 1) % DEPTH])
            ks[n][...] = entries(us[n][...], vs[n][...])
        return held[-2], held[-1], fetch_events(c + WIDE), give_events(c + WIDE)

    carry = (begin, begin, fetch_events(start), give_events(start))
    last, *_ = lax.fori_loop(lax.div(start, WIDE), steps // WIDE, step, carry)
    products(last, DEPTH - 1, ks[DEPTH - 1])
    for n, kind, (which, k) in sorted(after_loop, key=lambda late: (-late[2][0], late[0])):

        @pl.when(inside if kind else jnp.logical_not(inside))
        def _(which=which, k=k):
            (give_col if which else give_row)(k).start()

    total = own[...] + sums[0, :, cols(m)]
    for k in range(members):
        arrived(parts.at[members + k], precv.at[members + k])
        total = total + parts[members + k]
        if k:
            arrived(parts.at[mate(k)], precv.at[mate(k)])
            total = total + parts[mate(k)]
    out[...] = prb[...] + root * total
    for k in range(members):
        ask(k).wait_send()
        give_col(k).wait_send()
        if k:
            share(k).wait_send()
            give_row(k).wait_send()


def local(groups, members, points, counts, latent, probes):
    size = members * SH
    copies = 2 * members - 1
    return pl.pallas_call(
        functools.partial(kernel, groups, members),
        out_shape=jax.ShapeDtypeStruct(probes.shape, jnp.float32),
        in_specs=[pl.BlockSpec(memory_space=pl.ANY)] * 4,
        out_specs=pl.BlockSpec(memory_space=pltpu.VMEM),
        scratch_shapes=[
            pltpu.VMEM((8, SH), jnp.float32),
            pltpu.VMEM((1, SH), jnp.int32),
            pltpu.VMEM((1, SH), jnp.float32),
            pltpu.VMEM((16, SH), jnp.float32),
            pltpu.VMEM((2, members, 32, SH), jnp.bfloat16),
            pltpu.VMEM((2, size, FEAT), jnp.bfloat16),
            pltpu.VMEM((2, 2 * FEAT, size), jnp.bfloat16),
            pltpu.VMEM((2, 16, size), jnp.float32),
            pltpu.VMEM((2 * members, 16, SH), jnp.float32),
            pltpu.VMEM((16, SH), jnp.float32),
            *[pltpu.VMEM((BI, BJ), jnp.float32)] * (2 * DEPTH),
            *[pltpu.VMEM((BI, BJ), jnp.bfloat16)] * DEPTH,
            pltpu.SemaphoreType.DMA((4,)),
            pltpu.SemaphoreType.DMA((copies,)),
            pltpu.SemaphoreType.DMA((2, members)),
            pltpu.SemaphoreType.DMA((copies,)),
            pltpu.SemaphoreType.DMA((2 * members,)),
        ],
        compiler_params=pltpu.CompilerParams(
            collective_id=0, has_side_effects=True, vmem_limit_bytes=60 * 2**20
        ),
        cost_estimate=pl.CostEstimate(flops=10**10, bytes_accessed=10**7, transcendentals=10**8),
    )(points, counts.reshape(1, SH), latent.reshape(1, SH), probes)


def solution(mesh):
    spec = ("row", "col", "layer")
    groups = mesh.shape["row"] * 2
    members = mesh.shape["col"] // 2 * mesh.shape["layer"]
    return jax.shard_map(
        functools.partial(local, groups, members),
        mesh=mesh,
        in_specs=(P(None, spec), P(spec), P(spec), P(None, spec)),
        out_specs=P(None, spec),
        check_vma=False,
    )
```
